32 devices in a mesh: dp: 2 (over core), ctx: 16 (over z, y, x).
Axes of the slice: x: 2, y: 2, z: 4, core: 2. Of those that a mesh axis runs over, the one named last changes fastest.
Arguments:
- hidden_in: bfloat16 [4, 2048, 1024], P('dp', 'ctx'), may hold values from -6 to 6
- segments: int32 [4, 2048], P('dp'), may hold values from 0 to 10, as said below
- routes: int32 [4, 2048, 8], P('dp', 'ctx'), may hold values from 0 to 31, all different within a row; in each aligned block of 128 rows (0 to 127, 128 to 255, ..., all dimensions but the last counted through in order) at most 40 rows name the same one
- grad_out: bfloat16 [4, 2048, 1024], P('dp', 'ctx'), may hold values from -6 to 6
- gain_attn: bfloat16 [1024], P(('dp', 'ctx')), may hold values from 0.5 to 1.5
- w_query: bfloat16 [1024, 1024], P(('dp', 'ctx')), may hold values from -0.1875 to 0.1875
- w_key: bfloat16 [1024, 512], P(('dp', 'ctx')), may hold values from -0.1875 to 0.1875
- w_value: bfloat16 [1024, 512], P(('dp', 'ctx')), may hold values from -0.1875 to 0.1875
- w_out: bfloat16 [1024, 1024], P(('dp', 'ctx')), may hold values from -3 to 3
- gain_moe: bfloat16 [1024], P(('dp', 'ctx')), may hold values from 0.5 to 1.5
- w_router: bfloat16 [1024, 32], P(('dp', 'ctx')), may hold values from -0.09375 to 0.09375
- w_in: bfloat16 [32, 1024, 1024], P('ctx', 'dp'), may hold values from -0.1875 to 0.1875
- w_down: bfloat16 [32, 512, 1024], P('ctx', None, 'dp'), may hold values from -1 to 1
Outputs:
- output_hidden: bfloat16 [4, 2048, 1024], P('dp', 'ctx')
- grad_hidden: float32 [4, 2048, 1024], P('dp', 'ctx')
- grad_gain_attn: float32 [1024], P(('dp', 'ctx'))
- grad_query: float32 [1024, 1024], P(('dp', 'ctx'))
- grad_key: float32 [1024, 512], P(('dp', 'ctx'))
- grad_value: float32 [1024, 512], P(('dp', 'ctx'))
- grad_out_proj: float32 [1024, 1024], P(('dp', 'ctx'))
- grad_gain_moe: float32 [1024], P(('dp', 'ctx'))
- grad_router: float32 [1024, 32], P(('dp', 'ctx'))
- grad_in: float32 [32, 1024, 1024], P('ctx', 'dp')
- grad_down: float32 [32, 512, 1024], P('ctx', None, 'dp')
The draws below stay inside these ranges and needn't reach their ends.
Inputs may be any that keep to these rules, and one draw needn't show every extreme that they name: `segments`: segment numbers never fall along a sequence. Of sequences 2i and 2i + 1, one (drawn) is a single document numbered 2048 // 200; the other packs documents of 200 to 2000 positions numbered from 0, the last one possibly shorter. `routes`: each row names 8 different experts. In the 128 positions of one device of one sequence (aligned blocks), no expert is named more than 40 times.
All inputs are finite; a program needn't handle non-finite values.
Results may differ from the reference program's by a relative error of at most 0.024.
Values may be sent and summed in bfloat16 or wider, within the bound.
A program may use at most 192 MiB of HBM per device.

```python
import math
import jax
import jax.numpy as jnp
import numpy as np
from jax import lax

D = 1024
HEADS = 16
KV_HEADS = 8
HEAD_DIM = 64
FF = 512
EXPERTS = 32
TOP = 8
SPAN = 128
MICRO = 2
DOC_MIN = 200
DOC_MAX = 2000
SEQS = 4
SEQ_LEN = 2048
CAP = 40


def draw_segments(key, part):
    key = jax.random.fold_in(key, 17)
    first_key, second_key = jax.random.split(key)
    doc_count = SEQ_LEN // DOC_MIN + 1
    lengths = jax.random.randint(first_key, (SEQS, doc_count), DOC_MIN, DOC_MAX + 1)
    doc_ends = jnp.cumsum(lengths, axis=1)
    positions = jnp.arange(SEQ_LEN, dtype=jnp.int32)
    numbers = jnp.sum((doc_ends[:, None, :] <= positions[None, :, None]).astype(jnp.int32), -1)
    group_count = SEQS // MICRO
    whole_one = jax.random.randint(second_key, (group_count,), 0, MICRO)
    single = jnp.arange(SEQS, dtype=jnp.int32) % MICRO == jnp.repeat(whole_one, MICRO)
    return jnp.where(single[:, None], SEQ_LEN // DOC_MIN, numbers).astype(jnp.int32)


def block_scale(stream_key, extent, cuts, low, high):
    gain, own = 1.0, jax.random.fold_in(stream_key, 6)
    for dim, shards_of in cuts:
        draws = jnp.exp(jax.random.uniform(jax.random.fold_in(own, dim), (shards_of,), jnp.float32, low / len(cuts), high / len(cuts)))
        gain = gain * jnp.repeat(draws, extent[dim] // shards_of).reshape([-1 if axis == dim else 1 for axis in range(len(extent))])
    return gain


def routed_block(own_key, own, number, rows, amount, top, limit, slope):
    sequence = jax.random.permutation(own_key, amount)
    crowded, common = portions_of(amount, rows * top, limit, slope, True), portions_of(amount, rows * top, limit, slope, False)
    places = jnp.arange(amount)

    def named(sizes, turn):
        used = int((sizes > 0).sum())
        fixed = max(1, used // 4)
        moved = fixed + (places - fixed + turn * (used - fixed)) % max(1, amount - fixed)
        return jnp.zeros((amount,), jnp.int32).at[sequence[jnp.where(places < fixed, places, moved)]].set(jnp.asarray(sizes, jnp.int32))

    sizes = jnp.where(number % 4 == 0, named(crowded, number // 4), named(common, number - number // 4 - 1))
    mixed = jax.random.permutation(jax.random.fold_in(own, 3), amount)
    giver, receiver = mixed[0:amount // 2 * 2:2], mixed[1:amount // 2 * 2:2]
    room = jnp.minimum(sizes[giver] - 1, limit - sizes[receiver]) // 2
    room = jnp.where((giver == sequence[0]) | (receiver == sequence[0]) | (sizes[receiver] == 0), 0, jnp.maximum(room, 0))
    moved = jax.random.randint(jax.random.fold_in(own, 4), (amount // 2,), 0, 1 << 20) % (room + 1)
    sizes = sizes.at[giver].add(-moved).at[receiver].add(moved)
    items = jnp.searchsorted(jnp.cumsum(sizes), jnp.arange(rows * top), side="right").astype(jnp.int32)
    listing = items.reshape(top, rows).T
    listing = listing[jax.random.permutation(jax.random.fold_in(own, 1), rows)]
    turn = jax.random.randint(jax.random.fold_in(own, 2), (rows, 1), 0, top)
    return jnp.take_along_axis(listing, (jnp.arange(top)[None, :] + turn) % top, axis=1)


def portions_of(amount, total, reach, lean, full):
    portions = [(1 << 20) // math.isqrt(grade ** lean) + 1 for grade in range(1, amount + 1)]
    largest = reach if full else min(reach, max(-(-total // amount), total * portions[0] // sum(portions)))
    least = 1 if total - largest >= amount - 1 else 0
    given, rest = [largest] + [least] * (amount - 1), total - largest - least * (amount - 1)
    while rest > 0:
        free = [i for i in range(1, amount) if given[i] < largest] or [i for i in range(1, amount) if given[i] < reach]
        pool, left = sum([portions[i] for i in free]), rest
        for i in free:
            more = min(reach - given[i], max(1, left * portions[i] // pool), rest)
            given[i] = given[i] + more
            rest = rest - more
    return np.array(given)


def normal_values(rng, extent, deviation, most, shards=(), held_as=jnp.bfloat16):
    values = deviation * jax.random.normal(rng, extent, jnp.float32)
    if shards:
        values = values * block_scale(rng, extent, shards, -0.22, 0.18)
    return jnp.clip(values, -most, most).astype(held_as)


def setup_inputs(seed: int = 0) -> dict:
    key_of = jax.random.split(jax.random.key(seed), 14)
    hidden_in = normal_values(key_of[0], (SEQS, SEQ_LEN, D), 1.0, 6.0, ((0, 2), (1, 16)))
    segments = draw_segments(jax.random.fold_in(key_of[13], 71), 0)
    routes_keys = jax.random.split(jax.random.fold_in(key_of[2], 1), SEQS * SEQ_LEN // SPAN)
    routes_turns = jax.random.permutation(jax.random.fold_in(key_of[2], 3), SEQS * SEQ_LEN // SPAN)
    routes = jax.vmap(lambda own, number: routed_block(jax.random.fold_in(key_of[2], 2), own, number, SPAN, EXPERTS, TOP, CAP, 1))(routes_keys, routes_turns).reshape((SEQS, SEQ_LEN, TOP))
    grad_out = normal_values(key_of[3], (SEQS, SEQ_LEN, D), 1.0, 6.0, ((0, 2), (1, 16)))
    gain_attn = jnp.clip(1.0 + 0.1 * jax.random.normal(key_of[4], (D,), jnp.float32), 0.5, 1.5).astype(jnp.bfloat16)
    w_query = normal_values(key_of[5], (D, HEADS * HEAD_DIM), D ** -0.5, 0.1875, ((0, 32),))
    w_key = normal_values(key_of[6], (D, KV_HEADS * HEAD_DIM), D ** -0.5, 0.1875, ((0, 32),))
    w_value = normal_values(key_of[7], (D, KV_HEADS * HEAD_DIM), D ** -0.5, 0.1875, ((0, 32),))
    w_out = normal_values(key_of[8], (D, HEADS * HEAD_DIM), (max(D // 256, 1)) ** -0.5, 3.0, ((0, 32),))
    gain_moe = jnp.clip(1.0 + 0.1 * jax.random.normal(key_of[9], (D,), jnp.float32), 0.5, 1.5).astype(jnp.bfloat16)
    w_router = normal_values(key_of[10], (D, EXPERTS), (4 * D) ** -0.5, 0.09375, ((0, 32),))
    w_in = normal_values(key_of[11], (EXPERTS, D, 2 * FF), D ** -0.5, 0.1875, ((0, 16), (1, 2)))
    w_down = normal_values(key_of[12], (EXPERTS, FF, D), (max(FF // 16, 1)) ** -0.5, 1.0, ((0, 16), (2, 2)))
    return {"hidden_in": hidden_in, "segments": segments, "routes": routes, "grad_out": grad_out, "gain_attn": gain_attn, "w_query": w_query, "w_key": w_key, "w_value": w_value, "w_out": w_out, "gain_moe": gain_moe, "w_router": w_router, "w_in": w_in, "w_down": w_down}


EPS = 1e-06
ROPE_BASE = 10000.0
NEG = -1e+30
HIGH = lax.Precision.HIGHEST

@jax.custom_vjp
def low(v):
    return lax.optimization_barrier(v.astype(jnp.bfloat16)).astype(jnp.float32)

@jax.custom_vjp
def low_back(v):
    return v

def low_keep(v):
    return (low(v), None)

def low_pass(kept, grad):
    return (grad,)

def back_keep(v):
    return (v, None)

def back_low(kept, grad):
    return (low(grad),)
low.defvjp(low_keep, low_pass)
low_back.defvjp(back_keep, back_low)

def rope_tables(positions, head_dim):
    steps_f = jnp.arange(0, head_dim, 2, dtype=jnp.float32)
    inv_freq = jnp.exp(-math.log(ROPE_BASE) * steps_f / head_dim)
    angle = positions.astype(jnp.float32)[:, None] * inv_freq[None, :]
    cosine = jnp.concatenate([jnp.cos(angle), jnp.cos(angle)], -1)[:, None, :]
    sine_table = jnp.concatenate([jnp.sin(angle), jnp.sin(angle)], -1)[:, None, :]
    return (cosine, sine_table)

def rotate(tensor, cosine, sine_table):
    half = tensor.shape[-1] // 2
    turned = jnp.concatenate([-tensor[..., half:], tensor[..., :half]], -1)
    return tensor * cosine + turned * sine_table

def matmul(first_op, second_op):
    return jnp.dot(first_op, second_op, precision=HIGH)

def rms_normed(tensor, gain_vec):
    return tensor * lax.rsqrt(lax.optimization_barrier(jnp.mean(tensor * tensor, -1, keepdims=True)) + EPS) * gain_vec

def sequence_layer(params, inputs, seg_row, route_rows):
    gain_one, query_w, key_w, value_w, proj_w, gain_two, router_w, in_w, down_w = params
    length = inputs.shape[0]
    groups = HEADS // KV_HEADS
    score_scale = HEAD_DIM ** (-0.5)
    positions = jnp.arange(length, dtype=jnp.int32)
    cosine, sine_table = rope_tables(positions, HEAD_DIM)
    act_in = low(rms_normed(inputs, gain_one))
    query_raw = low_back(matmul(act_in, query_w))
    key_raw = low_back(matmul(act_in, key_w))
    values = low(low_back(matmul(act_in, value_w))).reshape(length, KV_HEADS, HEAD_DIM)
    queries = low(rotate(query_raw.reshape(length, HEADS, HEAD_DIM), cosine, sine_table))
    queries = queries.reshape(length, KV_HEADS, groups, HEAD_DIM)
    keys_rot = low(rotate(key_raw.reshape(length, KV_HEADS, HEAD_DIM), cosine, sine_table))
    block_size = math.gcd(length, 512)
    blocks = length // block_size

    def attend(inputs_block):
        query_block, pos_block, seg_block = inputs_block
        scores = low_back(jnp.einsum('qhgd,khd->hgqk', query_block, keys_rot, precision=HIGH) * score_scale)
        allowed = (positions[None, :] <= pos_block[:, None]) & (seg_row[None, :] == seg_block[:, None])
        weights_soft = jax.nn.softmax(jnp.where(allowed, scores, NEG), -1)
        return jnp.einsum('hgqk,khd->qhgd', low(weights_soft), values, precision=HIGH)
    attended = lax.map(jax.checkpoint(attend), (queries.reshape(blocks, block_size, KV_HEADS, groups, HEAD_DIM), positions.reshape(blocks, block_size), seg_row.reshape(blocks, block_size)))
    attended = low(low_back(attended.reshape(length, HEADS * HEAD_DIM)))
    resid = inputs + low_back(jnp.einsum('th,dh->td', attended, proj_w, precision=HIGH))
    moe_in = low(rms_normed(resid, gain_two))
    logits = low_back(matmul(moe_in, router_w))
    chosen = (route_rows[:, :, None] == jnp.arange(EXPERTS, dtype=jnp.int32)).astype(jnp.float32)
    selected = lax.optimization_barrier(jnp.sum(chosen * logits[:, None, :], -1))
    gate_weights = jax.nn.softmax(selected, -1)
    combine = lax.optimization_barrier(jnp.sum(gate_weights[:, :, None] * chosen, 1))

    def expert_step(running, expert_inputs):
        weight_in, weight_down, column = expert_inputs
        expert_in = low_back(moe_in)
        mixed_pre = low_back(matmul(expert_in, weight_in))
        product = low(jax.nn.silu(mixed_pre[:, :FF]) * mixed_pre[:, FF:])
        result = low(low_back(matmul(product, weight_down)))
        return (running + column[:, None] * result, None)
    moe_out, unused = lax.scan(jax.checkpoint(expert_step), jnp.zeros_like(resid), (in_w, down_w, combine.T))
    return resid + moe_out

def reference(hidden_in, segments, routes, grad_out, gain_attn, w_query, w_key, w_value, w_out, gain_moe, w_router, w_in, w_down):
    params = tuple((weight.astype(jnp.float32) for weight in (gain_attn, w_query, w_key, w_value, w_out, gain_moe, w_router, w_in, w_down)))

    def forward(inputs, weights):

        def one_sequence(seq_items):
            return sequence_layer(weights, seq_items[0], seq_items[1], seq_items[2])
        return lax.map(jax.checkpoint(one_sequence), (inputs, segments, routes))
    result, pullback = jax.vjp(forward, hidden_in.astype(jnp.float32), params)
    grad_input, grads = pullback(grad_out.astype(jnp.float32))
    return (result.astype(jnp.bfloat16), grad_input, grads[0], grads[1], grads[2], grads[3], grads[4], grads[5], grads[6], grads[7], grads[8])
```

```python
import math

import jax
import jax.numpy as jnp
from jax import lax
from jax.sharding import PartitionSpec as P

HEADS = 16
KV_HEADS = 8
HEAD_DIM = 64


EPS = 1e-06
ROPE_BASE = 10000.0
NEG = -1e30


def rope_tables(positions, head_dim):
    steps_f = jnp.arange(0, head_dim, 2, dtype=jnp.float32)
    inv_freq = jnp.exp(-math.log(ROPE_BASE) * steps_f / head_dim)
    angle = positions.astype(jnp.float32)[:, None] * inv_freq[None, :]
    cosine = jnp.concatenate([jnp.cos(angle), jnp.cos(angle)], -1)[:, None, :]
    sine_table = jnp.concatenate([jnp.sin(angle), jnp.sin(angle)], -1)[:, None, :]
    return (cosine, sine_table)


def rotate(tensor, cosine, sine_table):
    half = tensor.shape[-1] // 2
    turned = jnp.concatenate([-tensor[..., half:], tensor[..., :half]], -1)
    return tensor * cosine + turned * sine_table


def rotate_back(gradient, cosine, sine_table):
    half = gradient.shape[-1] // 2
    scaled = gradient * sine_table
    turned = jnp.concatenate([scaled[..., half:], -scaled[..., :half]], -1)
    return gradient * cosine + turned


def norm_back(gradient, normed, inverse, gain_vec):
    scaled = gradient * gain_vec
    return inverse * (scaled - normed * jnp.mean(scaled * normed, -1, keepdims=True))


def split_blocks(pieces):
    amount = pieces[0].shape[0]
    block_size = math.gcd(amount, 512)
    number = amount // block_size
    split_parts = tuple((piece.reshape((number, block_size) + piece.shape[1:]) for piece in pieces))
    starts = jnp.arange(number, dtype=jnp.int32) * block_size
    return (split_parts, starts, block_size)


def block_mask(key_start, block_size, query_pos, query_seg, seg_row):
    key_pos = key_start + jnp.arange(block_size, dtype=jnp.int32)
    key_seg = lax.dynamic_slice_in_dim(seg_row, key_start, block_size)
    return (key_pos[None, :] <= query_pos[:, None]) & (key_seg[None, :] == query_seg[:, None])


def attend_forward(carried, pieces, queries, query_pos, query_seg, seg_row, score_scale):
    kv_heads = queries.shape[1]
    head_dim = queries.shape[3]
    split_parts, starts, block_size = split_blocks(pieces)

    def one_block(run_state, block_inputs):
        run_max, run_sum, run_acc = run_state
        key_block, value_block, key_start = block_inputs
        key_heads = key_block.reshape(block_size, kv_heads, head_dim)
        value_heads = value_block.reshape(block_size, kv_heads, head_dim)
        allowed = block_mask(key_start, block_size, query_pos, query_seg, seg_row)
        scores = (
            jnp.einsum("qhgd,khd->hgqk", queries, key_heads, preferred_element_type=jnp.float32)
            * score_scale
        )
        new_max = jnp.maximum(run_max, jnp.max(jnp.where(allowed, scores, NEG), -1))
        factor = jnp.exp(run_max - new_max)
        weights_exp = jnp.where(allowed, jnp.exp(scores - new_max[..., None]), 0.0)
        run_sum = run_sum * factor + jnp.sum(weights_exp, -1)
        run_acc = run_acc * factor[..., None] + jnp.einsum(
            "hgqk,khd->hgqd",
            weights_exp.astype(jnp.bfloat16),
            value_heads,
            preferred_element_type=jnp.float32,
        )
        return ((new_max, run_sum, run_acc), None)

    final_state, unused = lax.scan(one_block, carried, (split_parts[0], split_parts[1], starts))
    return final_state


def attend_backward(
    carried,
    pieces,
    queries,
    query_pos,
    query_seg,
    seg_row,
    score_scale,
    grad_heads,
    log_sum,
    delta_rows,
):
    grad_query, grad_keys, grad_values = carried
    kv_heads = queries.shape[1]
    head_dim = queries.shape[3]
    split_parts, starts, block_size = split_blocks(pieces)

    def one_block(grad_acc, block_inputs):
        key_block, value_block, key_start = block_inputs
        key_heads = key_block.reshape(block_size, kv_heads, head_dim)
        value_heads = value_block.reshape(block_size, kv_heads, head_dim)
        allowed = block_mask(key_start, block_size, query_pos, query_seg, seg_row)
        scores = (
            jnp.einsum("qhgd,khd->hgqk", queries, key_heads, preferred_element_type=jnp.float32)
            * score_scale
        )
        probs_full = jnp.where(allowed, jnp.exp(scores - log_sum[..., None]), 0.0)
        grad_value = jnp.einsum(
            "hgqk,qhgd->khd",
            probs_full.astype(jnp.bfloat16),
            grad_heads,
            preferred_element_type=jnp.float32,
        )
        grad_prob = jnp.einsum(
            "qhgd,khd->hgqk", grad_heads, value_heads, preferred_element_type=jnp.float32
        )
        grad_score = (probs_full * (grad_prob - delta_rows[..., None])).astype(jnp.bfloat16)
        grad_acc = (
            grad_acc
            + jnp.einsum(
                "hgqk,khd->hgqd", grad_score, key_heads, preferred_element_type=jnp.float32
            )
            * score_scale
        )
        grad_key = (
            jnp.einsum("hgqk,qhgd->khd", grad_score, queries, preferred_element_type=jnp.float32)
            * score_scale
        )
        return (grad_acc, (grad_key.reshape(block_size, -1), grad_value.reshape(block_size, -1)))

    grad_query, (key_parts, value_parts) = lax.scan(
        one_block, grad_query, (split_parts[0], split_parts[1], starts)
    )
    kv_width = grad_keys.shape[1]
    grad_keys = key_parts.reshape(-1, kv_width)
    grad_values = value_parts.reshape(-1, kv_width)
    return (grad_query, grad_keys, grad_values)


def attention_forward(queries, keys_all, values_all, query_pos, query_segs, segments, score_scale):
    micro, span_len, kv_heads, groups, head_dim = queries.shape
    f32 = jnp.float32
    start_state = (
        jnp.full((kv_heads, groups, span_len), NEG, f32),
        jnp.zeros((kv_heads, groups, span_len), f32),
        jnp.zeros((kv_heads, groups, span_len, head_dim), f32),
    )

    def one(query_rows, key_rows, value_rows, query_seg, seg_row):
        return attend_forward(
            start_state,
            (key_rows, value_rows),
            query_rows,
            query_pos,
            query_seg,
            seg_row,
            score_scale,
        )

    run_max, run_sum, run_acc = jax.vmap(one)(
        queries, keys_all, values_all, query_segs, segments
    )
    return run_acc / run_sum[..., None], run_max + jnp.log(run_sum)


def attention_backward(
    queries,
    keys_all,
    values_all,
    query_pos,
    query_segs,
    segments,
    score_scale,
    grad_heads,
    log_sum,
    delta_rows,
):
    micro, span_len, kv_heads, groups, head_dim = queries.shape
    seq_len = segments.shape[1]
    f32 = jnp.float32
    back_state = (
        jnp.zeros((kv_heads, groups, span_len, head_dim), f32),
        jnp.zeros((seq_len, kv_heads * head_dim), f32),
        jnp.zeros((seq_len, kv_heads * head_dim), f32),
    )

    def one(query_rows, key_rows, value_rows, query_seg, seg_row, grad_rows, logs, deltas):
        return attend_backward(
            back_state,
            (key_rows, value_rows),
            query_rows,
            query_pos,
            query_seg,
            seg_row,
            score_scale,
            grad_rows,
            logs,
            deltas,
        )

    return jax.vmap(one)(
        queries, keys_all, values_all, query_segs, segments, grad_heads, log_sum, delta_rows
    )


def on_device(
    hidden_in,
    segments,
    routes,
    grad_out,
    gain_attn,
    w_query,
    w_key,
    w_value,
    w_out,
    gain_moe,
    w_router,
    w_in,
    w_down,
):
    span_len = hidden_in.shape[1]
    model_width = hidden_in.shape[2]
    ctx_size = lax.axis_size("ctx")
    my_index = lax.axis_index("ctx")
    exp_dev = w_in.shape[0]
    experts = exp_dev * ctx_size
    hidden = w_down.shape[1]
    top_count = routes.shape[2]
    capacity = span_len * top_count * 5 // (4 * experts)
    kv_heads = KV_HEADS
    head_dim = HEAD_DIM
    groups = HEADS // KV_HEADS
    kv_width = kv_heads * head_dim
    seq_len = segments.shape[1]
    score_scale = head_dim ** (-0.5)
    query_pos = my_index * span_len + jnp.arange(span_len, dtype=jnp.int32)
    cosine, sine_table = rope_tables(query_pos, head_dim)
    assigns = span_len * top_count
    expert_ids = jnp.arange(experts, dtype=jnp.int32)
    f32 = jnp.float32
    bf16 = jnp.bfloat16

    micro = hidden_in.shape[0]
    rows = micro * span_len
    dp_size = lax.axis_size("dp")
    qkv_width = w_query.shape[1] + 2 * kv_width
    q_width = w_query.shape[1]
    shard_rows = w_query.shape[0]
    used_width = qkv_width + w_out.shape[1] + experts + 2
    pack_width = -(-used_width // 128) * 128

    packed = jnp.concatenate(
        [
            w_query,
            w_key,
            w_value,
            w_out,
            w_router,
            gain_attn[:, None],
            gain_moe[:, None],
            jnp.zeros((shard_rows, pack_width - used_width), bf16),
        ],
        1,
    )
    packed = lax.all_gather(packed, ("dp", "ctx"), axis=0, tiled=True)
    qkv_full = packed[:, :qkv_width]
    proj_full = packed[:, qkv_width : qkv_width + w_out.shape[1]]
    tail = qkv_width + w_out.shape[1]
    router_full = packed[:, tail : tail + experts]
    gain_one = packed[:, tail + experts].astype(f32)
    gain_two = packed[:, tail + experts + 1].astype(f32)
    in_full = lax.all_gather(w_in, "dp", axis=1, tiled=True)
    down_full = lax.all_gather(w_down, "dp", axis=2, tiled=True)

    def exchange(block):
        return lax.all_to_all(block, "ctx", split_axis=0, concat_axis=0, tiled=True)

    route_rows = routes.reshape(rows, top_count)
    chosen = (route_rows[:, :, None] == expert_ids).astype(f32)
    has = jnp.sum(chosen, 1).astype(bf16).reshape(micro, span_len, experts)
    step = jnp.arange(span_len)
    earlier = (step[None, :] < step[:, None]).astype(bf16)
    rank = jnp.einsum("tu,mue->mte", earlier, has, preferred_element_type=f32)
    which = jnp.arange(micro, dtype=f32)[:, None, None] * capacity
    rank = (rank + which).reshape(rows, 1, experts)
    slots = micro * capacity
    rank_index = jnp.sum(chosen * rank, -1).astype(jnp.int32)
    slot_index = (route_rows * slots + rank_index).reshape(rows * top_count)
    total = rows * top_count
    sources = (
        jnp.full((experts * slots,), total, jnp.int32)
        .at[slot_index]
        .set(jnp.arange(total, dtype=jnp.int32))
    )
    token_src = sources // top_count
    padded_out = jnp.concatenate(
        [grad_out.reshape(rows, model_width), jnp.zeros((1, model_width), bf16)], 0
    )
    out_rows = padded_out[token_src].reshape(ctx_size, exp_dev, slots, model_width)
    recv_out = exchange(out_rows)

    cosine = jnp.tile(cosine, (micro, 1, 1))
    sine_table = jnp.tile(sine_table, (micro, 1, 1))
    inputs = hidden_in.reshape(rows, model_width).astype(f32)
    grad_final = grad_out.reshape(rows, model_width).astype(f32)
    inverse_one = lax.rsqrt(jnp.mean(inputs * inputs, -1, keepdims=True) + EPS)
    normed_one = inputs * inverse_one
    act_in = (normed_one * gain_one).astype(bf16)
    raw = jnp.dot(act_in, qkv_full, preferred_element_type=f32)
    queries = rotate(raw[:, :q_width].reshape(rows, HEADS, head_dim), cosine, sine_table)
    queries = queries.astype(bf16).reshape(micro, span_len, kv_heads, groups, head_dim)
    keys_low = rotate(
        raw[:, q_width : q_width + kv_width].reshape(rows, kv_heads, head_dim), cosine, sine_table
    )
    keys_low = keys_low.astype(bf16).reshape(micro, span_len, kv_width)
    values_low = raw[:, q_width + kv_width :].astype(bf16).reshape(micro, span_len, kv_width)
    kv_all = lax.all_gather(
        jnp.concatenate([keys_low, values_low], -1), "ctx", axis=1, tiled=True
    )
    keys_all = kv_all[..., :kv_width]
    values_all = kv_all[..., kv_width:]
    query_segs = lax.dynamic_slice_in_dim(segments, my_index * span_len, span_len, 1)
    attn_heads, log_sum = attention_forward(
        queries, keys_all, values_all, query_pos, query_segs, segments, score_scale
    )
    attn_rows = attn_heads.transpose(0, 3, 1, 2, 4).reshape(rows, HEADS * head_dim)
    attn_low = attn_rows.astype(bf16)
    resid = inputs + jnp.einsum("th,dh->td", attn_low, proj_full, preferred_element_type=f32)
    inverse_two = lax.rsqrt(jnp.mean(resid * resid, -1, keepdims=True) + EPS)
    normed_two = resid * inverse_two
    moe_in = (normed_two * gain_two).astype(bf16)
    logits = jnp.dot(moe_in, router_full, preferred_element_type=f32)
    selected = jnp.sum(chosen * logits[:, None, :], -1)
    gate_weights = jax.nn.softmax(selected, -1)
    padded_in = jnp.concatenate([moe_in, jnp.zeros((1, model_width), bf16)], 0)
    sent_rows = padded_in[token_src].reshape(ctx_size, exp_dev, slots, model_width)
    gate_slots = (
        jnp.zeros((experts * slots,), f32)
        .at[slot_index]
        .set(gate_weights.reshape(total))
        .reshape(ctx_size, exp_dev * slots)
    )
    recv_rows = exchange(sent_rows)
    recv_gates = exchange(gate_slots).reshape(ctx_size, exp_dev, slots, 1)
    recv_grads = (recv_gates * recv_out.astype(f32)).astype(bf16)
    mixed_pre = jnp.einsum("sepd,edf->sepf", recv_rows, in_full, preferred_element_type=f32)
    gate_part = mixed_pre[..., :hidden]
    up_part = mixed_pre[..., hidden:]
    sigmoid_gate = jax.nn.sigmoid(gate_part)
    swish_gate = gate_part * sigmoid_gate
    product = (swish_gate * up_part).astype(bf16)
    result = jnp.einsum("sepf,efd->sepd", product, down_full, preferred_element_type=f32)
    returned = exchange(result.astype(bf16))
    grad_prod = jnp.einsum("sepd,efd->sepf", recv_grads, down_full, preferred_element_type=f32)
    grad_mixed = jnp.concatenate(
        [
            grad_prod * up_part * sigmoid_gate * (1.0 + gate_part * (1.0 - sigmoid_gate)),
            grad_prod * swish_gate,
        ],
        -1,
    ).astype(bf16)
    grad_rows_in = jnp.einsum("sepf,edf->sepd", grad_mixed, in_full, preferred_element_type=f32)
    grad_back = exchange(grad_rows_in.astype(bf16)).reshape(experts * slots, model_width)
    acc_down = jnp.einsum("sepf,sepd->efd", product, recv_grads, preferred_element_type=f32)
    acc_in = jnp.einsum("sepd,sepf->edf", recv_rows, grad_mixed, preferred_element_type=f32)
    grad_in = lax.psum_scatter(acc_in.astype(bf16), "dp", scatter_dimension=1, tiled=True)
    grad_down = lax.psum_scatter(acc_down.astype(bf16), "dp", scatter_dimension=2, tiled=True)

    y_slots = returned.reshape(experts * slots, model_width)
    y_tokens = y_slots[slot_index].reshape(rows, top_count, model_width)
    moe_out = jnp.sum(gate_weights[:, :, None] * y_tokens, 1)
    output_hidden = (resid + moe_out).astype(bf16)
    grad_gate = jnp.sum(grad_final[:, None, :] * y_tokens, -1)
    grad_sel = gate_weights * (grad_gate - jnp.sum(gate_weights * grad_gate, -1, keepdims=True))
    grad_logit = jnp.sum(grad_sel[:, :, None] * chosen, 1).astype(bf16)
    acc_router = jnp.einsum("td,te->de", moe_in, grad_logit, preferred_element_type=f32)
    grad_moe_in = jnp.einsum("te,de->td", grad_logit, router_full, preferred_element_type=f32)
    grad_moe_in = grad_moe_in + jnp.sum(
        grad_back[slot_index].reshape(rows, top_count, model_width), 1, dtype=f32
    )
    acc_gain_two = jnp.sum(grad_moe_in * normed_two, 0)
    grad_resid = grad_final + norm_back(grad_moe_in, normed_two, inverse_two, gain_two)
    grad_attn_in = grad_resid.astype(bf16)
    acc_proj = jnp.einsum("td,th->dh", grad_attn_in, attn_low, preferred_element_type=f32)
    grad_attn_low = jnp.dot(grad_attn_in, proj_full, preferred_element_type=f32).astype(bf16)
    grad_heads = grad_attn_low.reshape(micro, span_len, kv_heads, groups, head_dim)
    delta_rows = jnp.sum(
        (grad_attn_low * attn_rows).reshape(micro, span_len, kv_heads, groups, head_dim), -1
    ).transpose(0, 2, 3, 1)
    grad_query, grad_keys, grad_values = attention_backward(
        queries,
        keys_all,
        values_all,
        query_pos,
        query_segs,
        segments,
        score_scale,
        grad_heads,
        log_sum,
        delta_rows,
    )
    grad_kv = jnp.concatenate([grad_keys.astype(bf16), grad_values.astype(bf16)], -1)
    grad_kv = grad_kv.reshape(micro, ctx_size, span_len, 2 * kv_width).transpose(1, 0, 2, 3)
    grad_kv = jnp.sum(exchange(grad_kv), 0, dtype=f32).reshape(rows, 2 * kv_width)
    query_turn = grad_query.transpose(0, 3, 1, 2, 4).reshape(rows, HEADS, head_dim)
    grad_q_raw = rotate_back(query_turn, cosine, sine_table).reshape(rows, q_width)
    grad_k_raw = rotate_back(
        grad_kv[:, :kv_width].reshape(rows, kv_heads, head_dim), cosine, sine_table
    ).reshape(rows, kv_width)
    grad_raw = jnp.concatenate(
        [grad_q_raw.astype(bf16), grad_k_raw.astype(bf16), grad_kv[:, kv_width:].astype(bf16)], 1
    )
    acc_qkv = jnp.einsum("td,th->dh", act_in, grad_raw, preferred_element_type=f32)
    grad_act = jnp.einsum("th,dh->td", grad_raw, qkv_full, preferred_element_type=f32)
    acc_gain_one = jnp.sum(grad_act * normed_one, 0)
    grad_hidden = grad_resid + norm_back(grad_act, normed_one, inverse_one, gain_one)

    def reduce_rows(block):
        width = block.shape[1]
        halves = block.reshape(dp_size, ctx_size * shard_rows, width)
        if dp_size == 2:
            mine = lax.axis_index("dp")
            away = lax.dynamic_index_in_dim(halves, 1 - mine, 0, keepdims=False).astype(bf16)
            got = lax.ppermute(away, "dp", [(0, 1), (1, 0)])
            half = lax.dynamic_index_in_dim(halves, mine, 0, keepdims=False) + got.astype(f32)
        else:
            half = lax.psum_scatter(halves, "dp", scatter_dimension=0, tiled=False)
        parts = exchange(half.astype(bf16).reshape(ctx_size, shard_rows, width))
        return jnp.sum(parts, 0, dtype=f32)

    early = reduce_rows(
        jnp.concatenate(
            [
                acc_proj,
                acc_router,
                acc_gain_two[:, None],
                jnp.zeros((model_width, 127 - experts % 128), f32),
            ],
            1,
        )
    )
    late = reduce_rows(
        jnp.concatenate([acc_qkv, acc_gain_one[:, None], jnp.zeros((model_width, 127), f32)], 1)
    )
    proj_width = w_out.shape[1]
    return (
        output_hidden.reshape(micro, span_len, model_width),
        grad_hidden.reshape(micro, span_len, model_width),
        late[:, qkv_width],
        late[:, :q_width],
        late[:, q_width : q_width + kv_width],
        late[:, q_width + kv_width : qkv_width],
        early[:, :proj_width],
        early[:, proj_width + experts],
        early[:, proj_width : proj_width + experts],
        grad_in.astype(f32),
        grad_down.astype(f32),
    )


def solution(mesh):
    placed = (
        P("dp", "ctx", None),
        P("dp", None),
        P("dp", "ctx", None),
        P("dp", "ctx", None),
        P(("dp", "ctx")),
        P(("dp", "ctx"), None),
        P(("dp", "ctx"), None),
        P(("dp", "ctx"), None),
        P(("dp", "ctx"), None),
        P(("dp", "ctx")),
        P(("dp", "ctx"), None),
        P("ctx", "dp", None),
        P("ctx", None, "dp"),
    )
    return jax.shard_map(
        on_device,
        mesh=mesh,
        in_specs=placed,
        out_specs=(
            P("dp", "ctx", None),
            P("dp", "ctx", None),
            P(("dp", "ctx")),
            P(("dp", "ctx"), None),
            P(("dp", "ctx"), None),
            P(("dp", "ctx"), None),
            P(("dp", "ctx"), None),
            P(("dp", "ctx")),
            P(("dp", "ctx"), None),
            P("ctx", "dp", None),
            P("ctx", None, "dp"),
        ),
        check_vma=False,
    )
```
